32 devices in a mesh: tp: 8 (over z, x), dp: 4 (over y, core).
Axes of the slice: x: 2, y: 2, z: 4, core: 2. Of those that a mesh axis runs over, the one named last changes fastest.
Arguments:
- hidden: bfloat16 [4096, 1600], P(('dp', 'tp')), parts along dimension 0
- gain: bfloat16 [1600], replicated, may hold values from 0.5 to 1.5
- head: bfloat16 [1600, 32000], P(None, 'tp')
- lengths: int32 [16], P('dp'), parts along dimension 0, may hold values from 64 to 256, as said below
- mask: int32 [4096], P(('dp', 'tp')), parts along dimension 0, may hold values 0 or 1
- targets: int32 [4096], P(('dp', 'tp')), parts along dimension 0, may hold values from 0 to 31999
Outputs:
- logprob: float32 [4096], P(('dp', 'tp')), parts along dimension 0
- entropy: float32 [4096], P(('dp', 'tp')), parts along dimension 0
The draws below stay inside these ranges and needn't reach their ends.
There are 4 independent parts, one for each index of `dp`. The reference program is written for one: setup_inputs(seed, part) draws one part's arguments, and reference() takes and returns one part's arrays. A program takes and returns all parts, laid end to end along the dimension named above; an argument that names none is the same for every part. Nothing has to cross between parts.
Inputs may be any that keep to these rules, and one draw needn't show every extreme that they name: `lengths`: each sequence's live length; the longest sequence of a batch fills all 256 slots.
All inputs are finite; a program needn't handle non-finite values. No bound on the sum of `mask` on one device may be relied on, other than what follows from the above.
Results may differ from the reference program's by a relative error of at most 0.003.
The reference program's roundings to bfloat16 on the way (of `normed`) count: a program that leaves them out, or rounds other values in their place, can miss the bound.
Values may be sent and summed in bfloat16 or wider, within the bound.
No kernel may reach another device: no remote copies, remote signals or barrier semaphores. Data moves between devices by JAX's collectives and lax.ppermute only.
A program may use at most 128 MiB of HBM per device.

```python
import math
import jax
import jax.numpy as jnp
import numpy as np
from jax import lax

D = 1600
VOCAB = 32000
SEQ_LEN = 256
TOKENS = 1024
SEQS = 4


def draw_hidden(key, part):
    k_base, k_rows, k_cols = jax.random.split(jax.random.fold_in(key, 11), 3)
    row_scale = jnp.exp(jax.random.uniform(k_rows, (TOKENS, 1), jnp.float32) * math.log(10.0))
    col_scale = jnp.exp(jax.random.uniform(k_cols, (1, D), jnp.float32) * math.log(10.0))
    base = jax.random.normal(k_base, (TOKENS, D), jnp.float32)
    values = base * row_scale * col_scale
    return values.astype(jnp.bfloat16)


def draw_head(key, part):
    k_base, k_cols = jax.random.split(jax.random.fold_in(key, 23), 2)
    cols = jnp.arange(VOCAB).astype(jnp.float32)
    col_scale = jnp.exp(jax.random.uniform(k_cols, (1, VOCAB), jnp.float32) * math.log(6.0)) * (1.0 + 2.0 * cols / VOCAB)[None, :]
    base = jax.random.normal(k_base, (D, VOCAB), jnp.float32)
    values = base * col_scale / jnp.sqrt(D * 1.0)
    return values.astype(jnp.bfloat16)


def draw_lengths(key, part):
    k_len, k_full = jax.random.split(jax.random.fold_in(key, 37))
    drawn = jax.random.randint(k_len, (SEQS,), SEQ_LEN // 4, SEQ_LEN + 1)
    full_at = jax.random.randint(k_full, (), 0, SEQS)
    return jnp.where(jnp.arange(SEQS) == full_at, SEQ_LEN, drawn).astype(jnp.int32)


def plant(entries, key, low, largest):
    shape = entries.shape
    index_at = [jax.random.randint(jax.random.fold_in(key, axis), (), 0, shape[axis]) for axis in range(len(shape))]
    entries = entries.at[tuple(index_at)].set(low)
    longest = shape.index(max(shape))
    index_at[longest] = (index_at[longest] + 1) % shape[longest]
    return entries.at[tuple(index_at)].set(largest)


def rank_table(number_of, skew):
    loads = [(1 << 20) // math.isqrt(grade ** skew) + 1 for grade in range(1, number_of + 1)]
    spread = 1 + sum(loads) // (1 << 30)
    return np.cumsum(np.array([max(1, weight // spread) for weight in loads]))


def ranked(key, shape, count, skew):
    listing = rank_table(count, skew)
    ticket = jax.random.randint(jax.random.fold_in(key, 1), shape, 0, int(listing[count - 1]))
    rank = jnp.searchsorted(jnp.asarray(listing, jnp.int32), ticket, side="right")
    return jax.random.permutation(jax.random.fold_in(key, 2), count)[rank].astype(jnp.int32)


def setup_inputs(seed: int = 0, part: int = 0) -> dict:
    key_list = jax.random.split(jax.random.key(seed), 7)
    part_splits = jax.random.split(jax.random.fold_in(key_list[6], part), 7)
    return {
        "hidden": draw_hidden(jax.random.fold_in(jax.random.fold_in(key_list[6], part), 71), part),
        "gain": jnp.clip(1.0 + 0.1 * jax.random.normal(key_list[1], (D,), jnp.float32), 0.5, 1.5).astype(jnp.bfloat16),
        "head": draw_head(jax.random.fold_in(key_list[6], 71), part),
        "lengths": draw_lengths(jax.random.fold_in(jax.random.fold_in(key_list[6], part), 71), part),
        "mask": plant((jax.random.randint(part_splits[4], (TOKENS,), 0, 4) < 3).astype(jnp.int32), jax.random.fold_in(part_splits[4], 1), 0, 1),
        "targets": plant(ranked(part_splits[5], (TOKENS,), VOCAB, 1), jax.random.fold_in(part_splits[5], 3), 0, VOCAB - 1).astype(jnp.int32),
    }


EPS = 1e-06

def reference(hidden, gain, head, lengths, mask, targets):
    xf = hidden.astype(jnp.float32)
    meansq = lax.optimization_barrier(jnp.mean(xf * xf, axis=-1, keepdims=True))
    normed = (xf * lax.rsqrt(meansq + EPS) * gain.astype(jnp.float32)).astype(jnp.bfloat16)
    headf = head.astype(jnp.float32)
    blocks = TOKENS // SEQ_LEN
    rows_b = normed.reshape(blocks, SEQ_LEN, D)
    tgt_b = targets.reshape(blocks, SEQ_LEN)

    def one_block(item):
        rows, tgt = item
        logits = jnp.dot(rows.astype(jnp.float32), headf)
        top = lax.optimization_barrier(jnp.max(logits, axis=-1))
        shifted = logits - top[:, None]
        expo = jnp.exp(shifted)
        total = lax.optimization_barrier(jnp.sum(expo, axis=-1))
        lse = top + jnp.log(total)
        picked = jnp.take_along_axis(logits, tgt[:, None].astype(jnp.int32), axis=1)[:, 0]
        logp = picked - lse
        ent = jnp.log(total) - lax.optimization_barrier(jnp.sum(expo * shifted, axis=-1)) / total
        return (logp, ent)
    logp, ent = lax.map(one_block, (rows_b, tgt_b))
    logp = logp.reshape(TOKENS)
    ent = ent.reshape(TOKENS)
    row_ids = jnp.arange(TOKENS, dtype=jnp.int32)
    slot = row_ids % SEQ_LEN
    seq_id = row_ids // SEQ_LEN
    seq_len = lengths.astype(jnp.int32)[seq_id]
    valid = (slot < seq_len) & (mask == 1)
    zero = jnp.zeros_like(logp)
    return (jnp.where(valid, logp, zero), jnp.where(valid, ent, zero))
```

```python
import functools

import jax
import jax.numpy as jnp
from jax import lax
from jax.experimental import pallas as pl
from jax.experimental.pallas import tpu as pltpu
from jax.sharding import PartitionSpec as P

SEQ_LEN = 256
EPS = 1e-06
EXTRA = 16
BASE = 256
VMEM_LIMIT = 32 * 1024 * 1024

VMEM = pl.BlockSpec(memory_space=pltpu.VMEM)
SMEM = pl.BlockSpec(memory_space=pltpu.SMEM)


def norm_kernel(me, lengths, hidden_t, gain, mask, targets, first, second, valid):
    width, rows = hidden_t.shape
    cut = first.shape[0] - EXTRA
    x = hidden_t[...].astype(jnp.float32)
    meansq = jnp.sum(x * x, axis=0, keepdims=True) * (1.0 / width)
    scale = lax.rsqrt(meansq + EPS)
    g = jnp.broadcast_to(gain[...].astype(jnp.float32), (rows, width)).T
    normed = (x * scale * g).astype(jnp.bfloat16)
    first[:cut, :] = normed[:cut]
    second[...] = normed[cut:]
    ids = targets[...]
    high = ids // BASE
    digit = lax.broadcasted_iota(jnp.int32, (EXTRA, rows), 0)
    digits = jnp.where(digit == 0, high, jnp.where(digit == 1, ids - high * BASE, 0))
    first[cut:, :] = digits.astype(jnp.float32).astype(jnp.bfloat16)
    row = me[0] * rows + lax.broadcasted_iota(jnp.int32, (1, rows), 1)
    length = jnp.zeros((1, rows), jnp.int32)
    for s in range(lengths.shape[0]):
        length = jnp.where(row // SEQ_LEN == s, lengths[s], length)
    live = (row % SEQ_LEN < length) & (mask[...] == 1)
    valid[...] = live.astype(jnp.int32)


def wave_kernel(blocks, me, head, *refs):
    parts = refs[: 2 * blocks]
    stats = refs[2 * blocks : 3 * blocks]
    x_scr, id_scr, logit_scr = refs[3 * blocks :]
    vocab = head.shape[1]
    rows = parts[0].shape[1]
    cut = parts[0].shape[0] - EXTRA
    for b in range(blocks):
        first, second = parts[2 * b], parts[2 * b + 1]
        at = pl.ds(b * rows, rows)
        x_scr[at, :cut] = first[:cut, :].T
        x_scr[at, cut:] = second[...].T
        digits = first[cut:, :].astype(jnp.float32).T.astype(jnp.int32)
        id_scr[at, :] = digits[:, 0:1] * BASE + digits[:, 1:2] - me[0] * vocab
    chunk = 512
    for lo in range(0, vocab, chunk):
        hi = min(vocab, lo + chunk)
        logit_scr[:, lo:hi] = jnp.dot(
            x_scr[...], head[:, lo:hi], preferred_element_type=jnp.float32
        )
    group = 16
    lane = lax.broadcasted_iota(jnp.int32, (group, 128), 1)
    col = lax.broadcasted_iota(jnp.int32, (group, vocab), 1)
    for b in range(blocks):
        found = []
        for g in range(rows // group):
            at = pl.ds(b * rows + g * group, group)
            logits = logit_scr[at, :]
            top = jnp.max(logits, axis=1, keepdims=True)
            shifted = logits - top
            expo = jnp.exp(shifted)
            sums = jnp.sum(expo, axis=1, keepdims=True)
            ent = jnp.sum(expo * shifted, axis=1, keepdims=True)
            hit = col == id_scr[at, :]
            tgt = jnp.sum(jnp.where(hit, logits, 0.0), axis=1, keepdims=True)
            found.append(
                jnp.where(
                    lane == 0,
                    top,
                    jnp.where(lane == 1, sums, jnp.where(lane == 2, ent, tgt)),
                )
            )
        stats[b][...] = jnp.concatenate(found, axis=0).T[:8, :]


def final_kernel(count, valid, *refs):
    stats, (logprob, entropy) = refs[:count], refs[count:]
    tops = [s[0:1, :] for s in stats]
    top = functools.reduce(jnp.maximum, tops)
    sums = ent = tgt = jnp.zeros_like(top)
    for s, own in zip(stats, tops):
        delta = own - top
        scale = jnp.exp(delta)
        own_sums = s[1:2, :]
        sums = sums + own_sums * scale
        ent = ent + (s[2:3, :] + delta * own_sums) * scale
        tgt = tgt + s[3:4, :]
    log_total = jnp.log(sums)
    live = valid[...] == 1
    logprob[...] = jnp.where(live, tgt - (top + log_total), 0.0)
    entropy[...] = jnp.where(live, log_total - ent / sums, 0.0)


def wave(me, head, blocks):
    count = len(blocks)
    width, vocab = head.shape
    rows = blocks[0][0].shape[1]
    return pl.pallas_call(
        functools.partial(wave_kernel, count),
        out_shape=[jax.ShapeDtypeStruct((8, rows), jnp.float32)] * count,
        in_specs=[SMEM, VMEM] + [VMEM] * (2 * count),
        out_specs=[VMEM] * count,
        scratch_shapes=[
            pltpu.VMEM((count * rows, width), jnp.bfloat16),
            pltpu.VMEM((count * rows, 1), jnp.int32),
            pltpu.VMEM((count * rows, vocab), jnp.float32),
        ],
        compiler_params=pltpu.CompilerParams(vmem_limit_bytes=VMEM_LIMIT),
        cost_estimate=pl.CostEstimate(
            flops=2 * count * rows * width * vocab,
            bytes_accessed=2 * width * vocab,
            transcendentals=count * rows * vocab,
        ),
        name=f"wave{count}",
    )(me, head, *[part for block in blocks for part in block])


def on_device(n, hidden, gain, head, lengths, mask, targets):
    rows, width = hidden.shape
    cut = (width // 2) // 128 * 128
    me = lax.axis_index("tp").astype(jnp.int32).reshape(1)

    ring = list(range(0, n, 2)) + list(range(1, n, 2))[::-1]

    def hop(value, by):
        pairs = [(ring[i], ring[(i + by) % n]) for i in range(n)]
        return lax.ppermute(value, "tp", pairs)

    first, second, valid = pl.pallas_call(
        norm_kernel,
        out_shape=[
            jax.ShapeDtypeStruct((cut + EXTRA, rows), jnp.bfloat16),
            jax.ShapeDtypeStruct((width - cut, rows), jnp.bfloat16),
            jax.ShapeDtypeStruct((1, rows), jnp.int32),
        ],
        in_specs=[SMEM, SMEM, VMEM, VMEM, VMEM, VMEM],
        out_specs=[VMEM] * 3,
        compiler_params=pltpu.CompilerParams(vmem_limit_bytes=VMEM_LIMIT),
        name="norm",
    )(me, lengths, hidden.T, gain.reshape(1, width), mask.reshape(1, rows), targets.reshape(1, rows))

    stats = []
    up = down = (first, second)
    held = [up]
    for step in range(1, n // 2 + 1):
        last = 2 * step == n
        if last:
            arrived = [(hop(up[0], 1), hop(down[1], -1))]
        else:
            up = (hop(up[0], 1), hop(up[1], 1))
            down_second = hop(down[1], -1)
            down = (hop(down[0], -1), down_second)
            arrived = [up, down]
        for k, s in enumerate(wave(me, head, held)):
            by = 0 if step == 1 else (1 - step, step - 1)[k]
            stats.append(hop(s, by) if by else s)
        held = arrived
    for k, s in enumerate(wave(me, head, held)):
        stats.append(hop(s, (-(n // 2), n // 2)[k]))

    logprob, entropy = pl.pallas_call(
        functools.partial(final_kernel, n),
        out_shape=[jax.ShapeDtypeStruct((1, rows), jnp.float32)] * 2,
        in_specs=[VMEM] * (n + 1),
        out_specs=[VMEM] * 2,
        name="combine",
    )(valid, *stats)
    return logprob.reshape(rows), entropy.reshape(rows)


def solution(mesh):
    return jax.shard_map(
        functools.partial(on_device, mesh.shape["tp"]),
        mesh=mesh,
        in_specs=(
            P(("dp", "tp"), None),
            P(),
            P(None, "tp"),
            P("dp"),
            P(("dp", "tp")),
            P(("dp", "tp")),
        ),
        out_specs=(P(("dp", "tp")), P(("dp", "tp"))),
        check_vma=False,
    )
```

```python
import functools

import jax
import jax.numpy as jnp
from jax import lax
from jax.experimental import pallas as pl
from jax.experimental.pallas import tpu as pltpu
from jax.sharding import PartitionSpec as P

SEQ_LEN = 256
EPS = 1e-06
EXTRA = 16
BASE = 256
VMEM_LIMIT = 32 * 1024 * 1024
NORM_LIMIT = 60 * 1024 * 1024
FINAL_LIMIT = 4 * 1024 * 1024
CHUNK = 512
GROUP = 16

VMEM = pl.BlockSpec(memory_space=pltpu.VMEM)
ANY = pl.BlockSpec(memory_space=pl.ANY)


def norm_kernel(hidden_any, gain_any, targets_any, lengths_any, mask_any, block, valid, *scratch):
    hidden_t, gain, targets, lengths, mask, sems = scratch
    width, rows = hidden_t.shape
    copies = [
        pltpu.make_async_copy(src, dst, sems.at[i])
        for i, (src, dst) in enumerate(
            [
                (hidden_any, hidden_t),
                (gain_any, gain),
                (targets_any, targets),
                (lengths_any, lengths),
                (mask_any, mask),
            ]
        )
    ]
    for copy in copies:
        copy.start()
    for copy in copies:
        copy.wait()
    x = hidden_t[...].astype(jnp.float32)
    meansq = jnp.sum(x * x, axis=0, keepdims=True) * (1.0 / width)
    scale = lax.rsqrt(meansq + EPS)
    g = jnp.broadcast_to(gain[...].astype(jnp.float32).reshape(1, width), (rows, width)).T
    block[:width, :] = (x * scale * g).astype(jnp.bfloat16)
    ids = targets[...].reshape(1, rows)
    high = ids // BASE
    digit = lax.broadcasted_iota(jnp.int32, (EXTRA, rows), 0)
    digits = jnp.where(digit == 0, high, jnp.where(digit == 1, ids - high * BASE, 0))
    block[width:, :] = digits.astype(jnp.float32).astype(jnp.bfloat16)
    row = lax.axis_index("tp") * rows + lax.broadcasted_iota(jnp.int32, (1, rows), 1)
    length = jnp.zeros((1, rows), jnp.int32)
    for s in range(lengths.shape[0]):
        length = jnp.where(row // SEQ_LEN == s, lengths[s], length)
    live = (row % SEQ_LEN < length) & (mask[...].reshape(1, rows) == 1)
    valid[...] = live.astype(jnp.int32)


def final_kernel(count, valid, *refs):
    stats, (logprob, entropy) = refs[:count], refs[count:]
    tops = [s[0:1, :] for s in stats]
    top = functools.reduce(jnp.maximum, tops)
    sums = ent = tgt = jnp.zeros_like(top)
    for s, own in zip(stats, tops):
        delta = own - top
        scale = jnp.exp(delta)
        own_sums = s[1:2, :]
        sums = sums + own_sums * scale
        ent = ent + (s[2:3, :] + delta * own_sums) * scale
        tgt = tgt + s[3:4, :]
    log_total = jnp.log(sums)
    live = valid[...] == 1
    logprob[...] = jnp.where(live, tgt - (top + log_total), 0.0)
    entropy[...] = jnp.where(live, log_total - ent / sums, 0.0)


def unpack(blocks, x_scr, id_scr, vocab):
    width = x_scr.shape[1]
    start = lax.axis_index("tp") * vocab
    for b, pieces in enumerate(blocks):
        rows = pieces[0].shape[1]
        at = pl.ds(b * rows, rows)
        low = 0
        for piece in pieces:
            high = min(low + piece.shape[0], width)
            x_scr[at, low:high] = piece[: high - low, :].T
            if piece.shape[0] > high - low:
                digits = piece[high - low :, :]
            low = high
        digits = digits.astype(jnp.float32).T.astype(jnp.int32)
        id_scr[at, :] = digits[:, 0:1] * BASE + digits[:, 1:2] - start


def chunks_of(vocab):
    return [(lo, min(vocab, lo + CHUNK)) for lo in range(0, vocab, CHUNK)]


def update(logits, lo, id_scr, acc):
    top_s, sum_s, ent_s, tgt_s = acc
    rows, wide = logits.shape
    tail = wide % 128
    if tail:
        pad = jnp.full((rows, 128 - tail), -jnp.inf, jnp.float32)
        logits = jnp.concatenate([logits, pad], axis=1)
    lane = lax.broadcasted_iota(jnp.int32, (GROUP, 128), 1)
    count = logits.shape[1] // 128
    for g in range(rows // GROUP):
        at = pl.ds(g * GROUP, GROUP)
        cols = [
            logits[g * GROUP : (g + 1) * GROUP, k * 128 : (k + 1) * 128] for k in range(count)
        ]
        top = functools.reduce(jnp.maximum, cols)
        if lo == 0:
            sums = ent = tgt = jnp.zeros((GROUP, 128), jnp.float32)
        else:
            old = top_s[at, :]
            top = jnp.maximum(old, top)
            delta = old - top
            scale = jnp.exp(delta)
            old_sums = sum_s[at, :]
            sums = old_sums * scale
            ent = (ent_s[at, :] + delta * old_sums) * scale
            tgt = tgt_s[at, :]
        ids = id_scr[at, :] - lo
        for k, col in enumerate(cols):
            shifted = col - top
            expo = jnp.exp(shifted)
            weighted = expo * shifted
            hit = lane == ids - k * 128
            if tail and k == count - 1:
                real = lane < tail
                expo = jnp.where(real, expo, 0.0)
                weighted = jnp.where(real, weighted, 0.0)
                hit = hit & real
            sums = sums + expo
            ent = ent + weighted
            tgt = jnp.where(hit, col, tgt)
        top_s[at, :] = top
        sum_s[at, :] = sums
        ent_s[at, :] = ent
        tgt_s[at, :] = tgt


def collect(stats, acc):
    top_s, sum_s, ent_s, tgt_s = acc
    for b, out in enumerate(stats):
        rows = out.shape[1]
        at = pl.ds(b * rows, rows)
        tops = top_s[at, :].T
        sums = sum_s[at, :].T
        ents = ent_s[at, :].T
        top = jnp.max(tops, axis=0, keepdims=True)
        delta = tops - top
        scale = jnp.exp(delta)
        out[0:1, :] = top
        out[1:2, :] = jnp.sum(sums * scale, axis=0, keepdims=True)
        out[2:3, :] = jnp.sum((ents + delta * sums) * scale, axis=0, keepdims=True)
        out[3:4, :] = jnp.sum(tgt_s[at, :].T, axis=0, keepdims=True)
        out[4:8, :] = jnp.zeros((4, rows), jnp.float32)


def wave_kernel(counts, head, *refs):
    blocks = []
    for count in counts:
        blocks.append(refs[:count])
        refs = refs[count:]
    stats, (x_scr, id_scr, *acc) = refs[: len(counts)], refs[len(counts) :]
    vocab = head.shape[1]
    unpack(blocks, x_scr, id_scr, vocab)
    for lo, hi in chunks_of(vocab):
        logits = jnp.dot(x_scr[...], head[:, lo:hi], preferred_element_type=jnp.float32)
        update(logits, lo, id_scr, acc)
    collect(stats, acc)


def own_kernel(head_any, block, stats, head, x_scr, id_scr, *rest):
    acc, sems = rest[:4], rest[4]
    vocab = head.shape[1]
    rows = stats.shape[1]
    spans = chunks_of(vocab)
    copies = [
        pltpu.make_async_copy(head_any.at[:, lo:hi], head.at[:, lo:hi], sems.at[i])
        for i, (lo, hi) in enumerate(spans)
    ]
    for copy in copies:
        copy.start()
    unpack([[block]], x_scr, id_scr, vocab)
    for (lo, hi), copy in zip(spans, copies):
        copy.wait()
        logits = jnp.dot(x_scr[...], head[:, lo:hi], preferred_element_type=jnp.float32)
        update(logits, lo, id_scr, acc)
    collect([stats], acc)


def wave_scratch(count, rows, width):
    return [
        pltpu.VMEM((count * rows, width), jnp.bfloat16),
        pltpu.VMEM((count * rows, 1), jnp.int32),
    ] + [pltpu.VMEM((count * rows, 128), jnp.float32)] * 4


def cost(rows, width, vocab):
    return pl.CostEstimate(
        flops=2 * rows * width * vocab,
        bytes_accessed=2 * width * vocab,
        transcendentals=rows * vocab,
    )


def wave(head, blocks):
    counts = [len(pieces) for pieces in blocks]
    width, vocab = head.shape
    rows = blocks[0][0].shape[1]
    return pl.pallas_call(
        functools.partial(wave_kernel, counts),
        out_shape=[jax.ShapeDtypeStruct((8, rows), jnp.float32)] * len(blocks),
        in_specs=[VMEM] * (1 + sum(counts)),
        out_specs=[VMEM] * len(blocks),
        scratch_shapes=wave_scratch(len(blocks), rows, width),
        compiler_params=pltpu.CompilerParams(vmem_limit_bytes=VMEM_LIMIT),
        cost_estimate=cost(len(blocks) * rows, width, vocab),
        name=f"wave{len(blocks)}",
    )(head, *[piece for pieces in blocks for piece in pieces])


def on_device(n, hidden, gain, head, lengths, mask, targets):
    rows, width = hidden.shape
    vocab = head.shape[1]
    cut = (width // 2) // 128 * 128

    ring = list(range(0, n, 2)) + list(range(1, n, 2))[::-1]

    def hop(value, by):
        pairs = [(ring[i], ring[(i + by) % n]) for i in range(n)]
        return lax.ppermute(value, "tp", pairs)

    block, valid = pl.pallas_call(
        norm_kernel,
        out_shape=[
            jax.ShapeDtypeStruct((width + EXTRA, rows), jnp.bfloat16),
            jax.ShapeDtypeStruct((1, rows), jnp.int32),
        ],
        in_specs=[ANY] * 5,
        out_specs=[VMEM] * 2,
        scratch_shapes=[
            pltpu.VMEM((width, rows), jnp.bfloat16),
            pltpu.VMEM((width,), jnp.bfloat16),
            pltpu.VMEM((rows,), jnp.int32),
            pltpu.SMEM(lengths.shape, jnp.int32),
            pltpu.VMEM((rows,), jnp.int32),
            pltpu.SemaphoreType.DMA((5,)),
        ],
        compiler_params=pltpu.CompilerParams(vmem_limit_bytes=NORM_LIMIT),
        name="norm",
    )(hidden.T, gain, targets, lengths, mask)

    own, head_near = pl.pallas_call(
        own_kernel,
        out_shape=[
            jax.ShapeDtypeStruct((8, rows), jnp.float32),
            jax.ShapeDtypeStruct(head.shape, head.dtype),
        ],
        in_specs=[ANY, VMEM],
        out_specs=[VMEM] * 2,
        scratch_shapes=wave_scratch(1, rows, width)
        + [pltpu.SemaphoreType.DMA((len(chunks_of(vocab)),))],
        compiler_params=pltpu.CompilerParams(vmem_limit_bytes=VMEM_LIMIT),
        cost_estimate=cost(rows, width, vocab),
        name="own",
    )(head, block)

    stats = [own]
    full = (n - 1) // 2
    up, down = hop(block, 1), hop(block, -1)
    up, down, head_near = lax.optimization_barrier((up, down, head_near))
    for step in range(2, full + 1):
        next_up, next_down = hop(up, 1), hop(down, -1)
        mine = wave(head_near, [[up], [down]])
        up, down, *mine = lax.optimization_barrier((next_up, next_down, *mine))
        stats += [hop(mine[0], 1 - step), hop(mine[1], step - 1)]
    if n % 2:
        mine = wave(head_near, [[up], [down]])
        stats += [hop(mine[0], -full), hop(mine[1], full)]
    else:
        halves = [hop(up[:cut], 1), hop(down[cut:], -1)]
        mine = wave(head_near, [[up], [down]])
        stats += [hop(mine[0], -full), hop(mine[1], full)]
        (far,) = wave(head_near, [halves])
        stats.append(hop(far, n // 2))

    logprob, entropy = pl.pallas_call(
        functools.partial(final_kernel, n),
        out_shape=[jax.ShapeDtypeStruct((1, rows), jnp.float32)] * 2,
        in_specs=[VMEM] * (n + 1),
        out_specs=[VMEM] * 2,
        compiler_params=pltpu.CompilerParams(vmem_limit_bytes=FINAL_LIMIT),
        name="combine",
    )(valid, *stats)
    return logprob.reshape(rows), entropy.reshape(rows)


def solution(mesh):
    return jax.shard_map(
        functools.partial(on_device, mesh.shape["tp"]),
        mesh=mesh,
        in_specs=(
            P(("dp", "tp"), None),
            P(),
            P(None, "tp"),
            P("dp"),
            P(("dp", "tp")),
            P(("dp", "tp")),
        ),
        out_specs=(P(("dp", "tp")), P(("dp", "tp"))),
        check_vma=False,
    )
```

```python
import functools

import jax
import jax.numpy as jnp
from jax import lax
from jax.experimental import pallas as pl
from jax.experimental.pallas import tpu as pltpu
from jax.sharding import PartitionSpec as P

SEQ_LEN = 256
EPS = 1e-06
EXTRA = 16
BASE = 256
VMEM_LIMIT = 32 * 1024 * 1024
NORM_LIMIT = 16 * 1024 * 1024
FINAL_LIMIT = 4 * 1024 * 1024
CHUNK = 512
GROUP = 16

VMEM = pl.BlockSpec(memory_space=pltpu.VMEM)
ANY = pl.BlockSpec(memory_space=pl.ANY)


def norm_kernel(hidden_any, gain_any, targets_any, lengths_any, mask_any, first, second, valid, *scratch):
    hidden_t, gain, targets, lengths, mask, sems = scratch
    width, rows = hidden_t.shape
    copies = [
        pltpu.make_async_copy(src, dst, sems.at[i])
        for i, (src, dst) in enumerate(
            [
                (hidden_any, hidden_t),
                (gain_any, gain),
                (targets_any, targets),
                (lengths_any, lengths),
                (mask_any, mask),
            ]
        )
    ]
    for copy in copies:
        copy.start()
    for copy in copies:
        copy.wait()
    x = hidden_t[...].astype(jnp.float32)
    meansq = jnp.sum(x * x, axis=0, keepdims=True) * (1.0 / width)
    scale = lax.rsqrt(meansq + EPS)
    g = jnp.broadcast_to(gain[...].astype(jnp.float32).reshape(1, width), (rows, width)).T
    normed = (x * scale * g).astype(jnp.bfloat16)
    cut = first.shape[0]
    first[...] = normed[:cut]
    second[: width - cut, :] = normed[cut:]
    ids = targets[...].reshape(1, rows)
    high = ids // BASE
    digit = lax.broadcasted_iota(jnp.int32, (EXTRA, rows), 0)
    digits = jnp.where(digit == 0, high, jnp.where(digit == 1, ids - high * BASE, 0))
    second[width - cut :, :] = digits.astype(jnp.float32).astype(jnp.bfloat16)
    row = lax.axis_index("tp") * rows + lax.broadcasted_iota(jnp.int32, (1, rows), 1)
    length = jnp.zeros((1, rows), jnp.int32)
    for s in range(lengths.shape[0]):
        length = jnp.where(row // SEQ_LEN == s, lengths[s], length)
    live = (row % SEQ_LEN < length) & (mask[...].reshape(1, rows) == 1)
    valid[...] = live.astype(jnp.int32)


def unpack(blocks, x_scr, id_scr, vocab):
    width = x_scr.shape[1]
    start = lax.axis_index("tp") * vocab
    for b, pieces in enumerate(blocks):
        rows = pieces[0].shape[1]
        at = pl.ds(b * rows, rows)
        low = 0
        for piece in pieces:
            high = min(low + piece.shape[0], width)
            x_scr[at, low:high] = piece[: high - low, :].T
            if piece.shape[0] > high - low:
                digits = piece[high - low :, :]
            low = high
        digits = digits.astype(jnp.float32).T.astype(jnp.int32)
        id_scr[at, :] = digits[:, 0:1] * BASE + digits[:, 1:2] - start


def chunks_of(vocab):
    return [(lo, min(vocab, lo + CHUNK)) for lo in range(0, vocab, CHUNK)]


def update(logits, lo, id_scr, acc):
    top_s, sum_s, ent_s, tgt_s = acc
    rows, wide = logits.shape
    tail = wide % 128
    if tail:
        pad = jnp.full((rows, 128 - tail), -jnp.inf, jnp.float32)
        logits = jnp.concatenate([logits, pad], axis=1)
    lane = lax.broadcasted_iota(jnp.int32, (GROUP, 128), 1)
    count = logits.shape[1] // 128
    for g in range(rows // GROUP):
        at = pl.ds(g * GROUP, GROUP)
        cols = [
            logits[g * GROUP : (g + 1) * GROUP, k * 128 : (k + 1) * 128] for k in range(count)
        ]
        top = functools.reduce(jnp.maximum, cols)
        if lo == 0:
            sums = ent = tgt = jnp.zeros((GROUP, 128), jnp.float32)
        else:
            old = top_s[at, :]
            top = jnp.maximum(old, top)
            delta = old - top
            scale = jnp.exp(delta)
            old_sums = sum_s[at, :]
            sums = old_sums * scale
            ent = (ent_s[at, :] + delta * old_sums) * scale
            tgt = tgt_s[at, :]
        ids = id_scr[at, :] - lo
        for k, col in enumerate(cols):
            shifted = col - top
            expo = jnp.exp(shifted)
            weighted = expo * shifted
            hit = lane == ids - k * 128
            if tail and k == count - 1:
                real = lane < tail
                expo = jnp.where(real, expo, 0.0)
                weighted = jnp.where(real, weighted, 0.0)
                hit = hit & real
            sums = sums + expo
            ent = ent + weighted
            tgt = jnp.where(hit, col, tgt)
        top_s[at, :] = top
        sum_s[at, :] = sums
        ent_s[at, :] = ent
        tgt_s[at, :] = tgt


def collect(stats, acc):
    top_s, sum_s, ent_s, tgt_s = acc
    for b, out in enumerate(stats):
        rows = out.shape[1]
        at = pl.ds(b * rows, rows)
        tops = top_s[at, :].T
        sums = sum_s[at, :].T
        ents = ent_s[at, :].T
        top = jnp.max(tops, axis=0, keepdims=True)
        delta = tops - top
        scale = jnp.exp(delta)
        out[0:1, :] = top
        out[1:2, :] = jnp.sum(sums * scale, axis=0, keepdims=True)
        out[2:3, :] = jnp.sum((ents + delta * sums) * scale, axis=0, keepdims=True)
        out[3:4, :] = jnp.sum(tgt_s[at, :].T, axis=0, keepdims=True)
        out[4:8, :] = jnp.zeros((4, rows), jnp.float32)


def wave_kernel(counts, head, *refs):
    blocks = []
    for count in counts:
        blocks.append(refs[:count])
        refs = refs[count:]
    stats, (x_scr, id_scr, *acc) = refs[: len(counts)], refs[len(counts) :]
    vocab = head.shape[1]
    unpack(blocks, x_scr, id_scr, vocab)
    for lo, hi in chunks_of(vocab):
        logits = jnp.dot(x_scr[...], head[:, lo:hi], preferred_element_type=jnp.float32)
        update(logits, lo, id_scr, acc)
    collect(stats, acc)


def last_wave_kernel(n, away, head, first, second, *refs):
    count = len(away)
    found, table, scratch = refs[:count], refs[count], refs[count + 1 :]
    wave_kernel([2], head, first, second, table.at[owner(n, n // 2)], *scratch)
    for places, stats in zip(away, found):
        table[owner(n, places)] = stats[...]


def owner(n, places):
    me = lax.axis_index("tp")
    half = (n + 1) // 2
    here = jnp.where(me % 2 == 0, me // 2, n - 1 - me // 2)
    there = (here + places + n) % n
    return jnp.where(there < half, 2 * there, 2 * (n - 1 - there) + 1)


def own_kernel(head_any, first, second, stats, head, x_scr, id_scr, *rest):
    acc, sems = rest[:4], rest[4]
    vocab = head.shape[1]
    rows = stats.shape[1]
    spans = chunks_of(vocab)
    copies = [
        pltpu.make_async_copy(head_any.at[:, lo:hi], head.at[:, lo:hi], sems.at[i])
        for i, (lo, hi) in enumerate(spans)
    ]
    for copy in copies:
        copy.start()
    unpack([[first, second]], x_scr, id_scr, vocab)
    for (lo, hi), copy in zip(spans, copies):
        copy.wait()
        logits = jnp.dot(x_scr[...], head[:, lo:hi], preferred_element_type=jnp.float32)
        update(logits, lo, id_scr, acc)
    collect([stats], acc)


def final_kernel(valid, shares, logprob, entropy):
    stats = [shares[i] for i in range(shares.shape[0])]
    tops = [s[0:1, :] for s in stats]
    top = functools.reduce(jnp.maximum, tops)
    sums = ent = tgt = jnp.zeros_like(top)
    for s, own in zip(stats, tops):
        delta = own - top
        scale = jnp.exp(delta)
        own_sums = s[1:2, :]
        sums = sums + own_sums * scale
        ent = ent + (s[2:3, :] + delta * own_sums) * scale
        tgt = tgt + s[3:4, :]
    log_total = jnp.log(sums)
    live = valid[...] == 1
    logprob[...] = jnp.where(live, tgt - (top + log_total), 0.0)
    entropy[...] = jnp.where(live, log_total - ent / sums, 0.0)


def wave_scratch(count, rows, width):
    return [
        pltpu.VMEM((count * rows, width), jnp.bfloat16),
        pltpu.VMEM((count * rows, 1), jnp.int32),
    ] + [pltpu.VMEM((count * rows, 128), jnp.float32)] * 4


def cost(rows, width, vocab):
    return pl.CostEstimate(
        flops=2 * rows * width * vocab,
        bytes_accessed=2 * width * vocab,
        transcendentals=rows * vocab,
    )


def wave(head, blocks):
    counts = [len(pieces) for pieces in blocks]
    width, vocab = head.shape
    rows = blocks[0][0].shape[1]
    return pl.pallas_call(
        functools.partial(wave_kernel, counts),
        out_shape=[jax.ShapeDtypeStruct((8, rows), jnp.float32)] * len(blocks),
        in_specs=[VMEM] * (1 + sum(counts)),
        out_specs=[VMEM] * len(blocks),
        scratch_shapes=wave_scratch(len(blocks), rows, width),
        compiler_params=pltpu.CompilerParams(vmem_limit_bytes=VMEM_LIMIT),
        cost_estimate=cost(len(blocks) * rows, width, vocab),
        name=f"wave{len(blocks)}",
    )(head, *[piece for pieces in blocks for piece in pieces])


def last_wave(n, head, pieces, found):
    width, vocab = head.shape
    rows = pieces[0].shape[1]
    return pl.pallas_call(
        functools.partial(last_wave_kernel, n, list(found)),
        out_shape=jax.ShapeDtypeStruct((n, 8, rows), jnp.float32),
        in_specs=[VMEM] * (3 + len(found)),
        out_specs=VMEM,
        scratch_shapes=wave_scratch(1, rows, width),
        compiler_params=pltpu.CompilerParams(vmem_limit_bytes=VMEM_LIMIT),
        cost_estimate=cost(rows, width, vocab),
        name="last",
    )(head, *pieces, *found.values())


def in_hbm(x):
    return pltpu.with_memory_space_constraint(x, pltpu.HBM)


def on_device(n, hidden, gain, head, lengths, mask, targets):
    rows, width = hidden.shape
    vocab = head.shape[1]
    cut = (width // 2) // 128 * 128

    ring = list(range(0, n, 2)) + list(range(1, n, 2))[::-1]

    def hop(value, by):
        pairs = [(ring[i], ring[(i + by) % n]) for i in range(n)]
        return lax.ppermute(value, "tp", pairs)

    *block, valid = pl.pallas_call(
        norm_kernel,
        out_shape=[
            jax.ShapeDtypeStruct((cut, rows), jnp.bfloat16),
            jax.ShapeDtypeStruct((width - cut + EXTRA, rows), jnp.bfloat16),
            jax.ShapeDtypeStruct((1, rows), jnp.int32),
        ],
        in_specs=[ANY] * 5,
        out_specs=[VMEM] * 3,
        scratch_shapes=[
            pltpu.VMEM((width, rows), jnp.bfloat16),
            pltpu.VMEM((width,), jnp.bfloat16),
            pltpu.VMEM((rows,), jnp.int32),
            pltpu.SMEM(lengths.shape, jnp.int32),
            pltpu.VMEM((rows,), jnp.int32),
            pltpu.SemaphoreType.DMA((5,)),
        ],
        compiler_params=pltpu.CompilerParams(vmem_limit_bytes=NORM_LIMIT),
        name="norm",
    )(*map(in_hbm, (hidden.T, gain, targets, lengths, mask)))

    own, head_near = pl.pallas_call(
        own_kernel,
        out_shape=[
            jax.ShapeDtypeStruct((8, rows), jnp.float32),
            jax.ShapeDtypeStruct(head.shape, head.dtype),
        ],
        in_specs=[ANY, VMEM, VMEM],
        out_specs=[VMEM] * 2,
        scratch_shapes=wave_scratch(1, rows, width)
        + [pltpu.SemaphoreType.DMA((len(chunks_of(vocab)),))],
        compiler_params=pltpu.CompilerParams(vmem_limit_bytes=VMEM_LIMIT),
        cost_estimate=cost(rows, width, vocab),
        name="own",
    )(in_hbm(head), *block)

    half = n // 2
    found = {0: own}
    up = [hop(piece, 1) for piece in block]
    down = [hop(piece, -1) for piece in block]
    up, down, head_near = lax.optimization_barrier((up, down, head_near))
    for step in range(1, half):
        if step < half - 1:
            next_up = [hop(piece, 1) for piece in up]
            next_down = [hop(piece, -1) for piece in down]
        else:
            next_up, next_down = [hop(up[0], 1)], [hop(down[1], -1)]
        found[-step], found[step] = wave(head_near, [up, down])
        if step < half - 1:
            for i in range(2):
                next_up[i], next_down[i], found[step] = lax.optimization_barrier(
                    (next_up[i], next_down[i], found[step])
                )
        else:
            next_up, next_down, found[step] = lax.optimization_barrier(
                (next_up, next_down, found[step])
            )
        up, down = next_up, next_down
    table = last_wave(n, head_near, up + down, found)

    shares = lax.all_to_all(table, "tp", 0, 0, tiled=True)
    logprob, entropy = pl.pallas_call(
        final_kernel,
        out_shape=[jax.ShapeDtypeStruct((1, rows), jnp.float32)] * 2,
        in_specs=[VMEM] * 2,
        out_specs=[VMEM] * 2,
        compiler_params=pltpu.CompilerParams(vmem_limit_bytes=FINAL_LIMIT),
        name="combine",
    )(valid, shares)
    return logprob.reshape(rows), entropy.reshape(rows)


def solution(mesh):
    return jax.shard_map(
        functools.partial(on_device, mesh.shape["tp"]),
        mesh=mesh,
        in_specs=(
            P(("dp", "tp"), None),
            P(),
            P(None, "tp"),
            P("dp"),
            P(("dp", "tp")),
            P(("dp", "tp")),
        ),
        out_specs=(P(("dp", "tp")), P(("dp", "tp"))),
        check_vma=False,
    )
```

```python
import functools

import jax
import jax.numpy as jnp
from jax import lax
from jax.experimental import pallas as pl
from jax.experimental.pallas import tpu as pltpu
from jax.sharding import PartitionSpec as P

SEQ_LEN = 256
EPS = 1e-06
EXTRA = 64
BASE = 256
VMEM_LIMIT = 32 * 1024 * 1024
NORM_LIMIT = 16 * 1024 * 1024
FINAL_LIMIT = 4 * 1024 * 1024
CHUNK = 512
GROUP = 16

VMEM = pl.BlockSpec(memory_space=pltpu.VMEM)
ANY = pl.BlockSpec(memory_space=pl.ANY)


def norm_kernel(hidden_any, gain_any, targets_any, lengths_any, mask_any, first, second, rest, place, *scratch):
    hidden_t, gain, targets, lengths, mask, sems = scratch
    width, rows = hidden_t.shape
    copies = [
        pltpu.make_async_copy(src, dst, sems.at[i])
        for i, (src, dst) in enumerate(
            [
                (hidden_any, hidden_t),
                (gain_any, gain),
                (targets_any, targets),
                (lengths_any, lengths),
                (mask_any, mask),
            ]
        )
    ]
    for copy in copies:
        copy.start()
    for copy in copies:
        copy.wait()
    row = lax.axis_index("tp") * rows + lax.broadcasted_iota(jnp.int32, (1, rows), 1)
    length = jnp.zeros((1, rows), jnp.int32)
    for s in range(lengths.shape[0]):
        length = jnp.where(row // SEQ_LEN == s, lengths[s], length)
    live = (row % SEQ_LEN < length) & (mask[...].reshape(1, rows) == 1)
    alive = jnp.where(live, 1.0, 0.0)
    down = lax.broadcasted_iota(jnp.int32, (rows, rows), 0)
    across = lax.broadcasted_iota(jnp.int32, (rows, rows), 1)
    before = jnp.where(down < across, 1.0, 0.0).astype(jnp.bfloat16)
    many = jnp.broadcast_to(alive, (16, rows)).astype(jnp.bfloat16)
    rank = jnp.dot(many, before, preferred_element_type=jnp.float32)[0:1]
    place[...] = jnp.where(live, rank, -1.0)
    select = (rank == down.astype(jnp.float32)) & live
    select = jnp.where(select, 1.0, 0.0).astype(jnp.bfloat16)

    x = hidden_t[...].astype(jnp.float32)
    meansq = jnp.sum(x * x, axis=0, keepdims=True) * (1.0 / width)
    scale = lax.rsqrt(meansq + EPS)
    g = jnp.broadcast_to(gain[...].astype(jnp.float32).reshape(1, width), (rows, width)).T
    normed = (x * scale * g).astype(jnp.bfloat16)
    ids = targets[...].reshape(1, rows)
    high = ids // BASE
    digit = lax.broadcasted_iota(jnp.int32, (EXTRA, rows), 0)
    digits = jnp.where(digit == 0, high, jnp.where(digit == 1, ids - high * BASE, 0))
    digits = jnp.where(digit == 2, jnp.sum(alive), digits.astype(jnp.float32))
    full = jnp.concatenate([normed, digits.astype(jnp.bfloat16)], axis=0)
    packed = lax.dot_general(
        select, full, (((1,), (1,)), ((), ())), preferred_element_type=jnp.float32
    ).astype(jnp.bfloat16)
    kept, cut = first.shape
    first[...] = packed[:kept, :cut]
    second[...] = packed[:kept, cut:]
    rest[...] = packed[kept:]


def unpack(blocks, x_scr, id_scr, vocab):
    width = x_scr.shape[1]
    shard = lax.axis_index("tp") * vocab
    counts = []
    for b, (first, second) in enumerate(blocks):
        rows, cut = first.shape
        at = pl.ds(b * rows, rows)
        x_scr[at, :cut] = first[...]
        x_scr[at, cut:] = second[:, : width - cut]
        low = (width - cut) // 128 * 128
        extra = second[:, low:].astype(jnp.float32)
        counts.append(jnp.max(extra[:, width - cut - low + 2 :][:, :1], axis=0, keepdims=True))
        extra = extra.astype(jnp.int32)
        digits = [extra[:, width - cut - low + i :][:, :1] for i in range(2)]
        id_scr[at, :] = digits[0] * BASE + digits[1] - shard
    return counts


def chunks_of(vocab):
    return [(lo, min(vocab, lo + CHUNK)) for lo in range(0, vocab, CHUNK)]


def update(logits, lo, id_scr, acc):
    top_s, sum_s, ent_s, tgt_s = acc
    rows, wide = logits.shape
    tail = wide % 128
    if tail:
        pad = jnp.full((rows, 128 - tail), -jnp.inf, jnp.float32)
        logits = jnp.concatenate([logits, pad], axis=1)
    lane = lax.broadcasted_iota(jnp.int32, (GROUP, 128), 1)
    count = logits.shape[1] // 128
    for g in range(rows // GROUP):
        at = pl.ds(g * GROUP, GROUP)
        cols = [
            logits[g * GROUP : (g + 1) * GROUP, k * 128 : (k + 1) * 128] for k in range(count)
        ]
        top = functools.reduce(jnp.maximum, cols)
        if lo == 0:
            sums = ent = tgt = jnp.zeros((GROUP, 128), jnp.float32)
        else:
            old = top_s[at, :]
            top = jnp.maximum(old, top)
            delta = old - top
            scale = jnp.exp(delta)
            old_sums = sum_s[at, :]
            sums = old_sums * scale
            ent = (ent_s[at, :] + delta * old_sums) * scale
            tgt = tgt_s[at, :]
        ids = id_scr[at, :] - lo
        for k, col in enumerate(cols):
            shifted = col - top
            expo = jnp.exp(shifted)
            weighted = expo * shifted
            hit = lane == ids - k * 128
            if tail and k == count - 1:
                real = lane < tail
                expo = jnp.where(real, expo, 0.0)
                weighted = jnp.where(real, weighted, 0.0)
                hit = hit & real
            sums = sums + expo
            ent = ent + weighted
            tgt = jnp.where(hit, col, tgt)
        top_s[at, :] = top
        sum_s[at, :] = sums
        ent_s[at, :] = ent
        tgt_s[at, :] = tgt


def collect(stats, rows, counts, acc):
    top_s, sum_s, ent_s, tgt_s = acc
    for b, (out, count) in enumerate(zip(stats, counts)):
        at = pl.ds(b * rows, rows)
        tops = top_s[at, :].T
        sums = sum_s[at, :].T
        ents = ent_s[at, :].T
        top = jnp.max(tops, axis=0, keepdims=True)
        delta = tops - top
        scale = jnp.exp(delta)
        out[0:1, :rows] = top
        out[1:2, :rows] = jnp.sum(sums * scale, axis=0, keepdims=True)
        out[2:3, :rows] = jnp.sum((ents + delta * sums) * scale, axis=0, keepdims=True)
        out[3:4, :rows] = jnp.sum(tgt_s[at, :].T, axis=0, keepdims=True)
        out[4:5, :] = jnp.broadcast_to(count, (1, out.shape[1]))
        out[5:8, :] = jnp.zeros((3, out.shape[1]), jnp.float32)


def wave_kernel(count, head, *refs):
    pieces, stats, (x_scr, id_scr, *acc) = refs[: 2 * count], refs[2 * count : 3 * count], refs[3 * count :]
    rows, vocab = pieces[0].shape[0], head.shape[1]
    counts = unpack(list(zip(pieces[::2], pieces[1::2])), x_scr, id_scr, vocab)
    for lo, hi in chunks_of(vocab):
        logits = jnp.dot(x_scr[...], head[:, lo:hi], preferred_element_type=jnp.float32)
        update(logits, lo, id_scr, acc)
    collect(stats, rows, counts, acc)


def last_wave_kernel(n, new, away, head, *refs):
    pieces, refs = refs[: 2 * new], refs[2 * new :]
    found, refs = refs[: len(away) - new], refs[len(away) - new :]
    table, most, *scratch = refs
    mine = [table.at[owner(n, places)] for places in away[:new]]
    wave_kernel(new, head, *pieces, *mine, *scratch)
    for places, stats in zip(away[new:], found):
        table[owner(n, places)] = stats[...]
    most[...] = functools.reduce(jnp.maximum, [table[i, 4:5, :] for i in range(n)])


def owner(n, places):
    me = lax.axis_index("tp")
    half = (n + 1) // 2
    here = jnp.where(me % 2 == 0, me // 2, n - 1 - me // 2)
    there = (here + places + n) % n
    return jnp.where(there < half, 2 * there, 2 * (n - 1 - there) + 1)


def own_kernel(head_any, first, second, stats, head, x_scr, id_scr, *rest):
    acc, sems = rest[:4], rest[4]
    vocab = head.shape[1]
    rows = stats.shape[1]
    spans = chunks_of(vocab)
    copies = [
        pltpu.make_async_copy(head_any.at[:, lo:hi], head.at[:, lo:hi], sems.at[i])
        for i, (lo, hi) in enumerate(spans)
    ]
    for copy in copies:
        copy.start()
    rows = first.shape[0]
    counts = unpack([(first, second)], x_scr, id_scr, vocab)
    for (lo, hi), copy in zip(spans, copies):
        copy.wait()
        logits = jnp.dot(x_scr[...], head[:, lo:hi], preferred_element_type=jnp.float32)
        update(logits, lo, id_scr, acc)
    collect([stats], rows, counts, acc)


def merge(shares):
    stats = [shares[i] for i in range(shares.shape[0])]
    tops = [s[0:1, :] for s in stats]
    top = functools.reduce(jnp.maximum, tops)
    sums = ent = tgt = jnp.zeros_like(top)
    for s, own in zip(stats, tops):
        delta = own - top
        scale = jnp.exp(delta)
        own_sums = s[1:2, :]
        sums = sums + own_sums * scale
        ent = ent + (s[2:3, :] + delta * own_sums) * scale
        tgt = tgt + s[3:4, :]
    log_total = jnp.log(sums)
    return tgt - (top + log_total), log_total - ent / sums


def final_kernel(kept, place, shares, more, logprob, entropy):
    rows = place.shape[1]
    down = lax.broadcasted_iota(jnp.int32, (rows, rows), 0)
    here = (down.astype(jnp.float32) == place[...]) & (down < kept)
    there = (down + kept).astype(jnp.float32) == place[...]
    for out, first, rest in zip((logprob, entropy), merge(shares), merge(more)):
        first = jnp.broadcast_to(first, (rows, rows)).T
        rest = jnp.broadcast_to(rest, (rows, rows)).T
        both = jnp.where(here, first, jnp.where(there, rest, 0.0))
        out[...] = jnp.sum(both, axis=0, keepdims=True)


def wave_scratch(count, rows, width):
    return [
        pltpu.VMEM((count * rows, width), jnp.bfloat16),
        pltpu.VMEM((count * rows, 1), jnp.int32),
    ] + [pltpu.VMEM((count * rows, 128), jnp.float32)] * 4


def cost(rows, width, vocab):
    return pl.CostEstimate(
        flops=2 * rows * width * vocab,
        bytes_accessed=2 * width * vocab,
        transcendentals=rows * vocab,
    )


def wave(head, blocks, lanes):
    count = len(blocks)
    width, vocab = head.shape
    rows = blocks[0][0].shape[0]
    return pl.pallas_call(
        functools.partial(wave_kernel, count),
        out_shape=[jax.ShapeDtypeStruct((8, lanes), jnp.float32)] * count,
        in_specs=[VMEM] * (1 + 2 * count),
        out_specs=[VMEM] * count,
        scratch_shapes=wave_scratch(count, rows, width),
        compiler_params=pltpu.CompilerParams(vmem_limit_bytes=VMEM_LIMIT),
        cost_estimate=cost(count * rows, width, vocab),
        name=f"wave{count}",
    )(head, *[piece for block in blocks for piece in block])


def last_wave(n, head, blocks, found, lanes):
    width, vocab = head.shape
    pieces = [piece for block in blocks.values() for piece in block]
    rows, new = pieces[0].shape[0], len(blocks)
    return pl.pallas_call(
        functools.partial(last_wave_kernel, n, new, [*blocks, *found]),
        out_shape=[
            jax.ShapeDtypeStruct((n, 8, lanes), jnp.float32),
            jax.ShapeDtypeStruct((1, lanes), jnp.float32),
        ],
        in_specs=[VMEM] * (1 + len(pieces) + len(found)),
        out_specs=[VMEM] * 2,
        scratch_shapes=wave_scratch(new, rows, width),
        compiler_params=pltpu.CompilerParams(vmem_limit_bytes=VMEM_LIMIT),
        cost_estimate=cost(new * rows, width, vocab),
        name=f"last{new}",
    )(head, *pieces, *found.values())


def in_hbm(x):
    return pltpu.with_memory_space_constraint(x, pltpu.HBM)


def on_device(n, hidden, gain, head, lengths, mask, targets):
    rows, width = hidden.shape
    vocab = head.shape[1]
    cut = (width // 2) // 128 * 128
    kept = rows * 7 // 8 // GROUP * GROUP

    ring = list(range(0, n, 2)) + list(range(1, n, 2))[::-1]

    def hop(value, by):
        pairs = [(ring[i], ring[(i + by) % n]) for i in range(n)]
        return lax.ppermute(value, "tp", pairs)

    *block, rest, place = pl.pallas_call(
        norm_kernel,
        out_shape=[
            jax.ShapeDtypeStruct((kept, cut), jnp.bfloat16),
            jax.ShapeDtypeStruct((kept, width - cut + EXTRA), jnp.bfloat16),
            jax.ShapeDtypeStruct((rows - kept, width + EXTRA), jnp.bfloat16),
            jax.ShapeDtypeStruct((1, rows), jnp.float32),
        ],
        in_specs=[ANY] * 5,
        out_specs=[VMEM] * 4,
        scratch_shapes=[
            pltpu.VMEM((width, rows), jnp.bfloat16),
            pltpu.VMEM((width,), jnp.bfloat16),
            pltpu.VMEM((rows,), jnp.int32),
            pltpu.SMEM(lengths.shape, jnp.int32),
            pltpu.VMEM((rows,), jnp.int32),
            pltpu.SemaphoreType.DMA((5,)),
        ],
        compiler_params=pltpu.CompilerParams(vmem_limit_bytes=NORM_LIMIT),
        name="norm",
    )(*map(in_hbm, (hidden.T, gain, targets, lengths, mask)))

    own, head_near = pl.pallas_call(
        own_kernel,
        out_shape=[
            jax.ShapeDtypeStruct((8, rows), jnp.float32),
            jax.ShapeDtypeStruct(head.shape, head.dtype),
        ],
        in_specs=[ANY, VMEM, VMEM],
        out_specs=[VMEM] * 2,
        scratch_shapes=wave_scratch(1, kept, width)
        + [pltpu.SemaphoreType.DMA((len(chunks_of(vocab)),))],
        compiler_params=pltpu.CompilerParams(vmem_limit_bytes=VMEM_LIMIT),
        cost_estimate=cost(kept, width, vocab),
        name="own",
    )(in_hbm(head), *block)

    half = n // 2
    found = {0: own}
    up = [hop(piece, 1) for piece in block]
    down = [hop(piece, -1) for piece in block]
    up, down, head_near = lax.optimization_barrier((up, down, head_near))
    for step in range(1, half):
        if step < half - 1:
            next_up = [hop(piece, 1) for piece in up]
            next_down = [hop(piece, -1) for piece in down]
        else:
            next_up, next_down = [hop(up[0], 1)], [hop(down[1], -1)]
        found[-step], found[step] = wave(head_near, [up, down], rows)
        if step < half - 1:
            for i in range(2):
                next_up[i], next_down[i], found[step] = lax.optimization_barrier(
                    (next_up[i], next_down[i], found[step])
                )
        else:
            next_up, next_down, found[step] = lax.optimization_barrier(
                (next_up, next_down, found[step])
            )
        up, down = next_up, next_down
    table, most = last_wave(n, head_near, {half: up + down}, found, rows)

    shares = lax.all_to_all(table, "tp", 0, 0, tiled=True)

    def others():
        blocks = {-k: (b[:, :cut], b[:, cut:]) for k, b in enumerate([rest] + [hop(rest, k) for k in range(1, n)])}
        table, _ = last_wave(n, head, blocks, {}, rows)
        return lax.all_to_all(table, "tp", 0, 0, tiled=True)

    more = lax.cond(most[0, 0] > kept, others, lambda: jnp.zeros_like(shares))
    logprob, entropy = pl.pallas_call(
        functools.partial(final_kernel, kept),
        out_shape=[jax.ShapeDtypeStruct((1, rows), jnp.float32)] * 2,
        in_specs=[VMEM] * 3,
        out_specs=[VMEM] * 2,
        compiler_params=pltpu.CompilerParams(vmem_limit_bytes=FINAL_LIMIT),
        name="combine",
    )(place, shares, more)
    return logprob.reshape(rows), entropy.reshape(rows)


def solution(mesh):
    return jax.shard_map(
        functools.partial(on_device, mesh.shape["tp"]),
        mesh=mesh,
        in_specs=(
            P(("dp", "tp"), None),
            P(),
            P(None, "tp"),
            P("dp"),
            P(("dp", "tp")),
            P(("dp", "tp")),
        ),
        out_specs=(P(("dp", "tp")), P(("dp", "tp"))),
        check_vma=False,
    )
```

```python
import functools

import jax
import jax.numpy as jnp
from jax import lax
from jax.experimental import pallas as pl
from jax.experimental.pallas import tpu as pltpu
from jax.sharding import PartitionSpec as P

SEQ_LEN = 256
EPS = 1e-06
EXTRA = 64
BASE = 256
VMEM_LIMIT = 32 * 1024 * 1024
NORM_LIMIT = 16 * 1024 * 1024
FINAL_LIMIT = 4 * 1024 * 1024
CHUNK = 512
GROUP = 16

VMEM = pl.BlockSpec(memory_space=pltpu.VMEM)
ANY = pl.BlockSpec(memory_space=pl.ANY)


def norm_kernel(hidden_any, gain_any, targets_any, lengths_any, mask_any, first, second, rest, place, *scratch):
    hidden_t, gain, targets, lengths, mask, sems = scratch
    width, rows = hidden_t.shape
    copies = [
        pltpu.make_async_copy(src, dst, sems.at[i])
        for i, (src, dst) in enumerate(
            [
                (hidden_any, hidden_t),
                (gain_any, gain),
                (targets_any, targets),
                (lengths_any, lengths),
                (mask_any, mask),
            ]
        )
    ]
    for copy in copies:
        copy.start()
    for copy in copies[1:]:
        copy.wait()
    row = lax.axis_index("tp") * rows + lax.broadcasted_iota(jnp.int32, (1, rows), 1)
    length = jnp.zeros((1, rows), jnp.int32)
    for s in range(lengths.shape[0]):
        length = jnp.where(row // SEQ_LEN == s, lengths[s], length)
    live = (row % SEQ_LEN < length) & (mask[...].reshape(1, rows) == 1)
    alive = jnp.where(live, 1.0, 0.0)
    down = lax.broadcasted_iota(jnp.int32, (rows, rows), 0)
    across = lax.broadcasted_iota(jnp.int32, (rows, rows), 1)
    before = jnp.where(down < across, 1.0, 0.0).astype(jnp.bfloat16)
    many = jnp.broadcast_to(alive, (16, rows)).astype(jnp.bfloat16)
    rank = jnp.dot(many, before, preferred_element_type=jnp.float32)[0:1]
    place[...] = jnp.where(live, rank, -1.0)
    select = (rank == down.astype(jnp.float32)) & live
    select = jnp.where(select, 1.0, 0.0).astype(jnp.bfloat16)

    g = jnp.broadcast_to(gain[...].astype(jnp.float32).reshape(1, width), (rows, width)).T
    ids = targets[...].reshape(1, rows)
    high = ids // BASE
    digit = lax.broadcasted_iota(jnp.int32, (EXTRA, rows), 0)
    digits = jnp.where(digit == 0, high, jnp.where(digit == 1, ids - high * BASE, 0))
    digits = jnp.where(digit == 2, jnp.sum(alive), digits.astype(jnp.float32))
    copies[0].wait()
    x = hidden_t[...].astype(jnp.float32)
    meansq = jnp.sum(x * x, axis=0, keepdims=True) * (1.0 / width)
    scale = lax.rsqrt(meansq + EPS)
    normed = (x * scale * g).astype(jnp.bfloat16)
    full = jnp.concatenate([normed, digits.astype(jnp.bfloat16)], axis=0)
    packed = lax.dot_general(
        select, full, (((1,), (1,)), ((), ())), preferred_element_type=jnp.float32
    ).astype(jnp.bfloat16)
    kept, cut = first.shape
    first[...] = packed[:kept, :cut]
    second[...] = packed[:kept, cut:]
    rest[...] = packed[kept:]


def unpack(blocks, x_scr, id_scr, vocab):
    width = x_scr.shape[1]
    shard = lax.axis_index("tp") * vocab
    counts = []
    for b, (first, second) in enumerate(blocks):
        rows, cut = first.shape
        at = pl.ds(b * rows, rows)
        x_scr[at, :cut] = first[...]
        x_scr[at, cut:] = second[:, : width - cut]
        low = (width - cut) // 128 * 128
        extra = second[:, low:].astype(jnp.float32)
        counts.append(jnp.max(extra[:, width - cut - low + 2 :][:, :1], axis=0, keepdims=True))
        extra = extra.astype(jnp.int32)
        digits = [extra[:, width - cut - low + i :][:, :1] for i in range(2)]
        id_scr[at, :] = digits[0] * BASE + digits[1] - shard
    return counts


def chunks_of(vocab):
    return [(lo, min(vocab, lo + CHUNK)) for lo in range(0, vocab, CHUNK)]


def update(logits, lo, id_scr, acc):
    top_s, sum_s, ent_s, tgt_s = acc
    rows, wide = logits.shape
    tail = wide % 128
    if tail:
        pad = jnp.full((rows, 128 - tail), -jnp.inf, jnp.float32)
        logits = jnp.concatenate([logits, pad], axis=1)
    lane = lax.broadcasted_iota(jnp.int32, (GROUP, 128), 1)
    count = logits.shape[1] // 128
    for g in range(rows // GROUP):
        at = pl.ds(g * GROUP, GROUP)
        cols = [
            logits[g * GROUP : (g + 1) * GROUP, k * 128 : (k + 1) * 128] for k in range(count)
        ]
        top = functools.reduce(jnp.maximum, cols)
        if lo == 0:
            sums = ent = tgt = jnp.zeros((GROUP, 128), jnp.float32)
        else:
            old = top_s[at, :]
            top = jnp.maximum(old, top)
            delta = old - top
            scale = jnp.exp(delta)
            old_sums = sum_s[at, :]
            sums = old_sums * scale
            ent = (ent_s[at, :] + delta * old_sums) * scale
            tgt = tgt_s[at, :]
        ids = id_scr[at, :] - lo
        for k, col in enumerate(cols):
            shifted = col - top
            expo = jnp.exp(shifted)
            weighted = expo * shifted
            hit = lane == ids - k * 128
            if tail and k == count - 1:
                real = lane < tail
                expo = jnp.where(real, expo, 0.0)
                weighted = jnp.where(real, weighted, 0.0)
                hit = hit & real
            sums = sums + expo
            ent = ent + weighted
            tgt = jnp.where(hit, col, tgt)
        top_s[at, :] = top
        sum_s[at, :] = sums
        ent_s[at, :] = ent
        tgt_s[at, :] = tgt


def collect(stats, rows, counts, acc):
    top_s, sum_s, ent_s, tgt_s = acc
    for b, (out, count) in enumerate(zip(stats, counts)):
        at = pl.ds(b * rows, rows)
        tops = top_s[at, :].T
        sums = sum_s[at, :].T
        ents = ent_s[at, :].T
        top = jnp.max(tops, axis=0, keepdims=True)
        delta = tops - top
        scale = jnp.exp(delta)
        out[0:1, :rows] = top
        out[1:2, :rows] = jnp.sum(sums * scale, axis=0, keepdims=True)
        out[2:3, :rows] = jnp.sum((ents + delta * sums) * scale, axis=0, keepdims=True)
        out[3:4, :rows] = jnp.sum(tgt_s[at, :].T, axis=0, keepdims=True)
        out[4:5, :] = jnp.broadcast_to(count, (1, out.shape[1]))
        out[5:8, :] = jnp.zeros((3, out.shape[1]), jnp.float32)


def wave_kernel(count, head, *refs):
    pieces, stats, (x_scr, id_scr, *acc) = refs[: 2 * count], refs[2 * count : 3 * count], refs[3 * count :]
    rows, vocab = pieces[0].shape[0], head.shape[1]
    counts = unpack(list(zip(pieces[::2], pieces[1::2])), x_scr, id_scr, vocab)
    for lo, hi in chunks_of(vocab):
        logits = jnp.dot(x_scr[...], head[:, lo:hi], preferred_element_type=jnp.float32)
        update(logits, lo, id_scr, acc)
    collect(stats, rows, counts, acc)


def last_wave_kernel(n, new, away, head, *refs):
    pieces, refs = refs[: 2 * new], refs[2 * new :]
    found, refs = refs[: len(away) - new], refs[len(away) - new :]
    table, most, *scratch = refs
    mine = [table.at[owner(n, places)] for places in away[:new]]
    wave_kernel(new, head, *pieces, *mine, *scratch)
    for places, stats in zip(away[new:], found):
        table[owner(n, places)] = stats[...]
    most[...] = functools.reduce(jnp.maximum, [table[i, 4:5, :] for i in range(n)])


def owner(n, places):
    me = lax.axis_index("tp")
    half = (n + 1) // 2
    here = jnp.where(me % 2 == 0, me // 2, n - 1 - me // 2)
    there = (here + places + n) % n
    return jnp.where(there < half, 2 * there, 2 * (n - 1 - there) + 1)


def own_kernel(head_any, first, second, stats, head, x_scr, id_scr, *rest):
    acc, sems = rest[:4], rest[4]
    vocab = head.shape[1]
    rows = stats.shape[1]
    spans = chunks_of(vocab)
    copies = [
        pltpu.make_async_copy(head_any.at[:, lo:hi], head.at[:, lo:hi], sems.at[i])
        for i, (lo, hi) in enumerate(spans)
    ]
    for copy in copies:
        copy.start()
    rows = first.shape[0]
    counts = unpack([(first, second)], x_scr, id_scr, vocab)
    for (lo, hi), copy in zip(spans, copies):
        copy.wait()
        logits = jnp.dot(x_scr[...], head[:, lo:hi], preferred_element_type=jnp.float32)
        update(logits, lo, id_scr, acc)
    collect([stats], rows, counts, acc)


def merge(shares):
    stats = [shares[i] for i in range(shares.shape[0])]
    tops = [s[0:1, :] for s in stats]
    top = functools.reduce(jnp.maximum, tops)
    sums = ent = tgt = jnp.zeros_like(top)
    for s, own in zip(stats, tops):
        delta = own - top
        scale = jnp.exp(delta)
        own_sums = s[1:2, :]
        sums = sums + own_sums * scale
        ent = ent + (s[2:3, :] + delta * own_sums) * scale
        tgt = tgt + s[3:4, :]
    log_total = jnp.log(sums)
    return tgt - (top + log_total), log_total - ent / sums


def final_kernel(kept, place, shares, more, logprob, entropy):
    rows = place.shape[1]
    down = lax.broadcasted_iota(jnp.int32, (rows, rows), 0)
    here = (down.astype(jnp.float32) == place[...]) & (down < kept)
    there = (down + kept).astype(jnp.float32) == place[...]
    for out, first, rest in zip((logprob, entropy), merge(shares), merge(more)):
        first = jnp.broadcast_to(first, (rows, rows)).T
        rest = jnp.broadcast_to(rest, (rows, rows)).T
        both = jnp.where(here, first, jnp.where(there, rest, 0.0))
        out[...] = jnp.sum(both, axis=0, keepdims=True)


def wave_scratch(count, rows, width):
    return [
        pltpu.VMEM((count * rows, width), jnp.bfloat16),
        pltpu.VMEM((count * rows, 1), jnp.int32),
    ] + [pltpu.VMEM((count * rows, 128), jnp.float32)] * 4


def cost(rows, width, vocab):
    return pl.CostEstimate(
        flops=2 * rows * width * vocab,
        bytes_accessed=2 * width * vocab,
        transcendentals=rows * vocab,
    )


def wave(head, blocks, lanes):
    count = len(blocks)
    width, vocab = head.shape
    rows = blocks[0][0].shape[0]
    return pl.pallas_call(
        functools.partial(wave_kernel, count),
        out_shape=[jax.ShapeDtypeStruct((8, lanes), jnp.float32)] * count,
        in_specs=[VMEM] * (1 + 2 * count),
        out_specs=[VMEM] * count,
        scratch_shapes=wave_scratch(count, rows, width),
        compiler_params=pltpu.CompilerParams(vmem_limit_bytes=VMEM_LIMIT),
        cost_estimate=cost(count * rows, width, vocab),
        name=f"wave{count}",
    )(head, *[piece for block in blocks for piece in block])


def last_wave(n, head, blocks, found, lanes):
    width, vocab = head.shape
    pieces = [piece for block in blocks.values() for piece in block]
    rows, new = pieces[0].shape[0], len(blocks)
    return pl.pallas_call(
        functools.partial(last_wave_kernel, n, new, [*blocks, *found]),
        out_shape=[
            jax.ShapeDtypeStruct((n, 8, lanes), jnp.float32),
            jax.ShapeDtypeStruct((1, lanes), jnp.float32),
        ],
        in_specs=[VMEM] * (1 + len(pieces) + len(found)),
        out_specs=[VMEM] * 2,
        scratch_shapes=wave_scratch(new, rows, width),
        compiler_params=pltpu.CompilerParams(vmem_limit_bytes=VMEM_LIMIT),
        cost_estimate=cost(new * rows, width, vocab),
        name=f"last{new}",
    )(head, *pieces, *found.values())


def in_hbm(x):
    return pltpu.with_memory_space_constraint(x, pltpu.HBM)


def on_device(n, hidden, gain, head, lengths, mask, targets):
    rows, width = hidden.shape
    vocab = head.shape[1]
    cut = (width // 2) // 128 * 128
    kept = rows * 7 // 8 // GROUP * GROUP

    ring = list(range(0, n, 2)) + list(range(1, n, 2))[::-1]

    def hop(value, by):
        pairs = [(ring[i], ring[(i + by) % n]) for i in range(n)]
        return lax.ppermute(value, "tp", pairs)

    *block, rest, place = pl.pallas_call(
        norm_kernel,
        out_shape=[
            jax.ShapeDtypeStruct((kept, cut), jnp.bfloat16),
            jax.ShapeDtypeStruct((kept, width - cut + EXTRA), jnp.bfloat16),
            jax.ShapeDtypeStruct((rows - kept, width + EXTRA), jnp.bfloat16),
            jax.ShapeDtypeStruct((1, rows), jnp.float32),
        ],
        in_specs=[ANY] * 5,
        out_specs=[VMEM] * 4,
        scratch_shapes=[
            pltpu.VMEM((width, rows), jnp.bfloat16),
            pltpu.VMEM((width,), jnp.bfloat16),
            pltpu.VMEM((rows,), jnp.int32),
            pltpu.SMEM(lengths.shape, jnp.int32),
            pltpu.VMEM((rows,), jnp.int32),
            pltpu.SemaphoreType.DMA((5,)),
        ],
        compiler_params=pltpu.CompilerParams(vmem_limit_bytes=NORM_LIMIT),
        name="norm",
    )(*map(in_hbm, (hidden.T, gain, targets, lengths, mask)))

    own, head_near = pl.pallas_call(
        own_kernel,
        out_shape=[
            jax.ShapeDtypeStruct((8, rows), jnp.float32),
            jax.ShapeDtypeStruct(head.shape, head.dtype),
        ],
        in_specs=[ANY, VMEM, VMEM],
        out_specs=[VMEM] * 2,
        scratch_shapes=wave_scratch(1, kept, width)
        + [pltpu.SemaphoreType.DMA((len(chunks_of(vocab)),))],
        compiler_params=pltpu.CompilerParams(vmem_limit_bytes=VMEM_LIMIT),
        cost_estimate=cost(kept, width, vocab),
        name="own",
    )(in_hbm(head), *block)

    half = n // 2
    found = {0: own}
    up = [hop(piece, 1) for piece in block]
    down = [hop(piece, -1) for piece in block]
    up, down, head_near = lax.optimization_barrier((up, down, head_near))
    for step in range(1, half):
        if step < half - 1:
            next_up = [hop(piece, 1) for piece in up]
            next_down = [hop(piece, -1) for piece in down]
        else:
            next_up, next_down = [hop(up[0], 1)], [hop(down[1], -1)]
        found[-step], found[step] = wave(head_near, [up, down], rows)
        if step < half - 1:
            for i in range(2):
                next_up[i], next_down[i], found[step] = lax.optimization_barrier(
                    (next_up[i], next_down[i], found[step])
                )
        else:
            next_up, next_down, found[step] = lax.optimization_barrier(
                (next_up, next_down, found[step])
            )
        up, down = next_up, next_down
    table, most = last_wave(n, head_near, {half: up + down}, found, rows)

    shares = lax.all_to_all(table, "tp", 0, 0, tiled=True)

    def others():
        blocks = {-k: (b[:, :cut], b[:, cut:]) for k, b in enumerate([rest] + [hop(rest, k) for k in range(1, n)])}
        table, _ = last_wave(n, head, blocks, {}, rows)
        return lax.all_to_all(table, "tp", 0, 0, tiled=True)

    more = lax.cond(most[0, 0] > kept, others, lambda: jnp.zeros_like(shares))
    logprob, entropy = pl.pallas_call(
        functools.partial(final_kernel, kept),
        out_shape=[jax.ShapeDtypeStruct((1, rows), jnp.float32)] * 2,
        in_specs=[VMEM] * 3,
        out_specs=[VMEM] * 2,
        compiler_params=pltpu.CompilerParams(vmem_limit_bytes=FINAL_LIMIT),
        name="combine",
    )(place, shares, more)
    return logprob.reshape(rows), entropy.reshape(rows)


def solution(mesh):
    return jax.shard_map(
        functools.partial(on_device, mesh.shape["tp"]),
        mesh=mesh,
        in_specs=(
            P(("dp", "tp"), None),
            P(),
            P(None, "tp"),
            P("dp"),
            P(("dp", "tp")),
            P(("dp", "tp")),
        ),
        out_specs=(P(("dp", "tp")), P(("dp", "tp"))),
        check_vma=False,
    )
```

```python
import functools

import jax
import jax.numpy as jnp
from jax import lax
from jax.experimental import pallas as pl
from jax.experimental.pallas import tpu as pltpu
from jax.sharding import PartitionSpec as P

SEQ_LEN = 256
EPS = 1e-06
EXTRA = 64
BASE = 256
VMEM_LIMIT = 32 * 1024 * 1024
NORM_LIMIT = 16 * 1024 * 1024
FINAL_LIMIT = 4 * 1024 * 1024
CHUNK = 512
GROUP = 16

VMEM = pl.BlockSpec(memory_space=pltpu.VMEM)
ANY = pl.BlockSpec(memory_space=pl.ANY)


def norm_kernel(hidden_any, gain_any, targets_any, lengths_any, mask_any, first, second, rest, place, *scratch):
    hidden_t, gain, targets, lengths, mask, sems = scratch
    width, rows = hidden_t.shape
    copies = [
        pltpu.make_async_copy(src, dst, sems.at[i])
        for i, (src, dst) in enumerate(
            [
                (hidden_any, hidden_t),
                (gain_any, gain),
                (targets_any, targets),
                (lengths_any, lengths),
                (mask_any, mask),
            ]
        )
    ]
    for copy in copies:
        copy.start()
    for copy in copies:
        copy.wait()
    row = lax.axis_index("tp") * rows + lax.broadcasted_iota(jnp.int32, (1, rows), 1)
    length = jnp.zeros((1, rows), jnp.int32)
    for s in range(lengths.shape[0]):
        length = jnp.where(row // SEQ_LEN == s, lengths[s], length)
    live = (row % SEQ_LEN < length) & (mask[...].reshape(1, rows) == 1)
    alive = jnp.where(live, 1.0, 0.0)
    down = lax.broadcasted_iota(jnp.int32, (rows, rows), 0)
    across = lax.broadcasted_iota(jnp.int32, (rows, rows), 1)
    before = jnp.where(down < across, 1.0, 0.0).astype(jnp.bfloat16)
    many = jnp.broadcast_to(alive, (16, rows)).astype(jnp.bfloat16)
    rank = jnp.dot(many, before, preferred_element_type=jnp.float32)[0:1]
    place[...] = jnp.where(live, rank, -1.0)
    select = (rank == down.astype(jnp.float32)) & live
    select = jnp.where(select, 1.0, 0.0).astype(jnp.bfloat16)

    x = hidden_t[...].astype(jnp.float32)
    meansq = jnp.sum(x * x, axis=0, keepdims=True) * (1.0 / width)
    scale = lax.rsqrt(meansq + EPS)
    g = jnp.broadcast_to(gain[...].astype(jnp.float32).reshape(1, width), (rows, width)).T
    normed = (x * scale * g).astype(jnp.bfloat16)
    ids = targets[...].reshape(1, rows)
    high = ids // BASE
    digit = lax.broadcasted_iota(jnp.int32, (EXTRA, rows), 0)
    digits = jnp.where(digit == 0, high, jnp.where(digit == 1, ids - high * BASE, 0))
    digits = jnp.where(digit == 2, jnp.sum(alive), digits.astype(jnp.float32))
    full = jnp.concatenate([normed, digits.astype(jnp.bfloat16)], axis=0)
    packed = lax.dot_general(
        select, full, (((1,), (1,)), ((), ())), preferred_element_type=jnp.float32
    ).astype(jnp.bfloat16)
    kept, cut = first.shape
    first[...] = packed[:kept, :cut]
    second[...] = packed[:kept, cut:]
    rest[...] = packed[kept:]


def unpack(blocks, x_scr, id_scr, vocab):
    width = x_scr.shape[1]
    shard = lax.axis_index("tp") * vocab
    counts = []
    for b, (first, second) in enumerate(blocks):
        rows, cut = first.shape
        at = pl.ds(b * rows, rows)
        x_scr[at, :cut] = first[...]
        x_scr[at, cut:] = second[:, : width - cut]
        low = (width - cut) // 128 * 128
        extra = second[:, low:].astype(jnp.float32)
        counts.append(jnp.max(extra[:, width - cut - low + 2 :][:, :1], axis=0, keepdims=True))
        extra = extra.astype(jnp.int32)
        digits = [extra[:, width - cut - low + i :][:, :1] for i in range(2)]
        id_scr[at, :] = digits[0] * BASE + digits[1] - shard
    return counts


def chunks_of(vocab):
    return [(lo, min(vocab, lo + CHUNK)) for lo in range(0, vocab, CHUNK)]


def update(logits, lo, id_scr, acc):
    top_s, sum_s, ent_s, tgt_s = acc
    rows, wide = logits.shape
    tail = wide % 128
    if tail:
        pad = jnp.full((rows, 128 - tail), -jnp.inf, jnp.float32)
        logits = jnp.concatenate([logits, pad], axis=1)
    lane = lax.broadcasted_iota(jnp.int32, (GROUP, 128), 1)
    count = logits.shape[1] // 128
    for g in range(rows // GROUP):
        at = pl.ds(g * GROUP, GROUP)
        cols = [
            logits[g * GROUP : (g + 1) * GROUP, k * 128 : (k + 1) * 128] for k in range(count)
        ]
        top = functools.reduce(jnp.maximum, cols)
        if lo == 0:
            sums = ent = tgt = jnp.zeros((GROUP, 128), jnp.float32)
        else:
            old = top_s[at, :]
            top = jnp.maximum(old, top)
            delta = old - top
            scale = jnp.exp(delta)
            old_sums = sum_s[at, :]
            sums = old_sums * scale
            ent = (ent_s[at, :] + delta * old_sums) * scale
            tgt = tgt_s[at, :]
        ids = id_scr[at, :] - lo
        for k, col in enumerate(cols):
            shifted = col - top
            expo = jnp.exp(shifted)
            weighted = expo * shifted
            hit = lane == ids - k * 128
            if tail and k == count - 1:
                real = lane < tail
                expo = jnp.where(real, expo, 0.0)
                weighted = jnp.where(real, weighted, 0.0)
                hit = hit & real
            sums = sums + expo
            ent = ent + weighted
            tgt = jnp.where(hit, col, tgt)
        top_s[at, :] = top
        sum_s[at, :] = sums
        ent_s[at, :] = ent
        tgt_s[at, :] = tgt


def collect(stats, rows, counts, acc):
    top_s, sum_s, ent_s, tgt_s = acc
    for b, (out, count) in enumerate(zip(stats, counts)):
        at = pl.ds(b * rows, rows)
        tops = top_s[at, :].T
        sums = sum_s[at, :].T
        ents = ent_s[at, :].T
        top = jnp.max(tops, axis=0, keepdims=True)
        delta = tops - top
        scale = jnp.exp(delta)
        out[0:1, :rows] = top
        out[1:2, :rows] = jnp.sum(sums * scale, axis=0, keepdims=True)
        out[2:3, :rows] = jnp.sum((ents + delta * sums) * scale, axis=0, keepdims=True)
        out[3:4, :rows] = jnp.sum(tgt_s[at, :].T, axis=0, keepdims=True)
        out[4:5, :] = jnp.broadcast_to(count, (1, out.shape[1]))
        out[5:8, :] = jnp.zeros((3, out.shape[1]), jnp.float32)


def wave_kernel(count, head, *refs):
    pieces, stats, (x_scr, id_scr, *acc) = refs[: 2 * count], refs[2 * count : 3 * count], refs[3 * count :]
    rows, vocab = pieces[0].shape[0], head.shape[1]
    counts = unpack(list(zip(pieces[::2], pieces[1::2])), x_scr, id_scr, vocab)
    for lo, hi in chunks_of(vocab):
        logits = jnp.dot(x_scr[...], head[:, lo:hi], preferred_element_type=jnp.float32)
        update(logits, lo, id_scr, acc)
    collect(stats, rows, counts, acc)


def last_wave_kernel(n, new, away, head, *refs):
    pieces, refs = refs[: 2 * new], refs[2 * new :]
    found, refs = refs[: len(away) - new], refs[len(away) - new :]
    table, most, *scratch = refs
    mine = [table.at[owner(n, places)] for places in away[:new]]
    wave_kernel(new, head, *pieces, *mine, *scratch)
    for places, stats in zip(away[new:], found):
        table[owner(n, places)] = stats[...]
    most[...] = functools.reduce(jnp.maximum, [table[i, 4:5, :] for i in range(n)])


def owner(n, places):
    me = lax.axis_index("tp")
    half = (n + 1) // 2
    here = jnp.where(me % 2 == 0, me // 2, n - 1 - me // 2)
    there = (here + places + n) % n
    return jnp.where(there < half, 2 * there, 2 * (n - 1 - there) + 1)


def own_kernel(head_any, first, second, stats, head, x_scr, id_scr, *rest):
    acc, sems = rest[:4], rest[4]
    vocab = head.shape[1]
    rows = stats.shape[1]
    spans = chunks_of(vocab)
    copies = [
        pltpu.make_async_copy(head_any.at[:, lo:hi], head.at[:, lo:hi], sems.at[i])
        for i, (lo, hi) in enumerate(spans)
    ]
    for copy in copies:
        copy.start()
    rows = first.shape[0]
    counts = unpack([(first, second)], x_scr, id_scr, vocab)
    for (lo, hi), copy in zip(spans, copies):
        copy.wait()
        logits = jnp.dot(x_scr[...], head[:, lo:hi], preferred_element_type=jnp.float32)
        update(logits, lo, id_scr, acc)
    collect([stats], rows, counts, acc)


def merge(shares):
    stats = [shares[i] for i in range(shares.shape[0])]
    tops = [s[0:1, :] for s in stats]
    top = functools.reduce(jnp.maximum, tops)
    sums = ent = tgt = jnp.zeros_like(top)
    for s, own in zip(stats, tops):
        delta = own - top
        scale = jnp.exp(delta)
        own_sums = s[1:2, :]
        sums = sums + own_sums * scale
        ent = ent + (s[2:3, :] + delta * own_sums) * scale
        tgt = tgt + s[3:4, :]
    log_total = jnp.log(sums)
    return tgt - (top + log_total), log_total - ent / sums


def final_kernel(kept, place, shares, more, logprob, entropy):
    rows = place.shape[1]
    down = lax.broadcasted_iota(jnp.int32, (rows, rows), 0)
    here = down.astype(jnp.float32) == place[...]
    for out, first, rest in zip((logprob, entropy), merge(shares), merge(more)):
        both = jnp.concatenate([first[:, :kept], rest[:, : rows - kept]], axis=1)
        both = jnp.broadcast_to(both, (rows, rows)).T
        out[...] = jnp.sum(jnp.where(here, both, 0.0), axis=0, keepdims=True)


def wave_scratch(count, rows, width):
    return [
        pltpu.VMEM((count * rows, width), jnp.bfloat16),
        pltpu.VMEM((count * rows, 1), jnp.int32),
    ] + [pltpu.VMEM((count * rows, 128), jnp.float32)] * 4


def cost(rows, width, vocab):
    return pl.CostEstimate(
        flops=2 * rows * width * vocab,
        bytes_accessed=2 * width * vocab,
        transcendentals=rows * vocab,
    )


def wave(head, blocks, lanes):
    count = len(blocks)
    width, vocab = head.shape
    rows = blocks[0][0].shape[0]
    return pl.pallas_call(
        functools.partial(wave_kernel, count),
        out_shape=[jax.ShapeDtypeStruct((8, lanes), jnp.float32)] * count,
        in_specs=[VMEM] * (1 + 2 * count),
        out_specs=[VMEM] * count,
        scratch_shapes=wave_scratch(count, rows, width),
        compiler_params=pltpu.CompilerParams(vmem_limit_bytes=VMEM_LIMIT),
        cost_estimate=cost(count * rows, width, vocab),
        name=f"wave{count}",
    )(head, *[piece for block in blocks for piece in block])


def last_wave(n, head, blocks, found, lanes):
    width, vocab = head.shape
    pieces = [piece for block in blocks.values() for piece in block]
    rows, new = pieces[0].shape[0], len(blocks)
    return pl.pallas_call(
        functools.partial(last_wave_kernel, n, new, [*blocks, *found]),
        out_shape=[
            jax.ShapeDtypeStruct((n, 8, lanes), jnp.float32),
            jax.ShapeDtypeStruct((1, lanes), jnp.float32),
        ],
        in_specs=[VMEM] * (1 + len(pieces) + len(found)),
        out_specs=[VMEM] * 2,
        scratch_shapes=wave_scratch(new, rows, width),
        compiler_params=pltpu.CompilerParams(vmem_limit_bytes=VMEM_LIMIT),
        cost_estimate=cost(new * rows, width, vocab),
        name=f"last{new}",
    )(head, *pieces, *found.values())


def in_hbm(x):
    return pltpu.with_memory_space_constraint(x, pltpu.HBM)


def on_device(n, hidden, gain, head, lengths, mask, targets):
    rows, width = hidden.shape
    vocab = head.shape[1]
    cut = (width // 2) // 128 * 128
    kept = rows * 7 // 8 // GROUP * GROUP

    ring = list(range(0, n, 2)) + list(range(1, n, 2))[::-1]

    def hop(value, by):
        pairs = [(ring[i], ring[(i + by) % n]) for i in range(n)]
        return lax.ppermute(value, "tp", pairs)

    *block, rest, place = pl.pallas_call(
        norm_kernel,
        out_shape=[
            jax.ShapeDtypeStruct((kept, cut), jnp.bfloat16),
            jax.ShapeDtypeStruct((kept, width - cut + EXTRA), jnp.bfloat16),
            jax.ShapeDtypeStruct((rows - kept, width + EXTRA), jnp.bfloat16),
            jax.ShapeDtypeStruct((1, rows), jnp.float32),
        ],
        in_specs=[ANY] * 5,
        out_specs=[VMEM] * 4,
        scratch_shapes=[
            pltpu.VMEM((width, rows), jnp.bfloat16),
            pltpu.VMEM((width,), jnp.bfloat16),
            pltpu.VMEM((rows,), jnp.int32),
            pltpu.SMEM(lengths.shape, jnp.int32),
            pltpu.VMEM((rows,), jnp.int32),
            pltpu.SemaphoreType.DMA((5,)),
        ],
        compiler_params=pltpu.CompilerParams(vmem_limit_bytes=NORM_LIMIT),
        name="norm",
    )(*map(in_hbm, (hidden.T, gain, targets, lengths, mask)))

    own, head_near = pl.pallas_call(
        own_kernel,
        out_shape=[
            jax.ShapeDtypeStruct((8, rows), jnp.float32),
            jax.ShapeDtypeStruct(head.shape, head.dtype),
        ],
        in_specs=[ANY, VMEM, VMEM],
        out_specs=[VMEM] * 2,
        scratch_shapes=wave_scratch(1, kept, width)
        + [pltpu.SemaphoreType.DMA((len(chunks_of(vocab)),))],
        compiler_params=pltpu.CompilerParams(vmem_limit_bytes=VMEM_LIMIT),
        cost_estimate=cost(kept, width, vocab),
        name="own",
    )(in_hbm(head), *block)

    half = n // 2
    found = {0: own}
    up = [hop(piece, 1) for piece in block]
    down = [hop(piece, -1) for piece in block]
    up, down, head_near = lax.optimization_barrier((up, down, head_near))
    for step in range(1, half):
        if step < half - 1:
            next_up = [hop(piece, 1) for piece in up]
            next_down = [hop(piece, -1) for piece in down]
        else:
            next_up, next_down = [hop(up[0], 1)], [hop(down[1], -1)]
        found[-step], found[step] = wave(head_near, [up, down], rows)
        if step < half - 1:
            for i in range(2):
                next_up[i], next_down[i], found[step] = lax.optimization_barrier(
                    (next_up[i], next_down[i], found[step])
                )
        else:
            next_up, next_down, found[step] = lax.optimization_barrier(
                (next_up, next_down, found[step])
            )
        up, down = next_up, next_down
    table, most = last_wave(n, head_near, {half: up + down}, found, rows)

    shares = lax.all_to_all(table, "tp", 0, 0, tiled=True)

    def others():
        blocks = {-k: (b[:, :cut], b[:, cut:]) for k, b in enumerate([rest] + [hop(rest, k) for k in range(1, n)])}
        table, _ = last_wave(n, head, blocks, {}, rows)
        return lax.all_to_all(table, "tp", 0, 0, tiled=True)

    more = lax.cond(most[0, 0] > kept, others, lambda: jnp.zeros_like(shares))
    logprob, entropy = pl.pallas_call(
        functools.partial(final_kernel, kept),
        out_shape=[jax.ShapeDtypeStruct((1, rows), jnp.float32)] * 2,
        in_specs=[VMEM] * 3,
        out_specs=[VMEM] * 2,
        compiler_params=pltpu.CompilerParams(vmem_limit_bytes=FINAL_LIMIT),
        name="combine",
    )(place, shares, more)
    return logprob.reshape(rows), entropy.reshape(rows)


def solution(mesh):
    return jax.shard_map(
        functools.partial(on_device, mesh.shape["tp"]),
        mesh=mesh,
        in_specs=(
            P(("dp", "tp"), None),
            P(),
            P(None, "tp"),
            P("dp"),
            P(("dp", "tp")),
            P(("dp", "tp")),
        ),
        out_specs=(P(("dp", "tp")), P(("dp", "tp"))),
        check_vma=False,
    )
```
